32 devices in a mesh: groups: 2 (over y), dp: 4 (over z), mp: 4 (over x, core).
Axes of the slice: x: 2, y: 2, z: 4, core: 2. Of those that a mesh axis runs over, the one named last changes fastest.
Arguments:
- embeddings: bfloat16 [16384, 1024], P(('groups', 'dp')), parts along dimension 0, may hold values from -60 to 60
- rotation: bfloat16 [1024, 1024], P(None, 'mp'), may hold values from -0.1875 to 0.1875
- codes: int32 [2, 16384, 16], P(None, ('groups', 'dp'), 'mp'), parts along dimension 1, may hold values from 0 to 255
Outputs:
- centroids: bfloat16 [512, 1024], P('groups', 'mp'), parts along dimension 0
- new_rotation: float32 [2048, 1024], P(('groups', 'dp'), 'mp'), parts along dimension 0
- rotated: bfloat16 [16384, 1024], P(('groups', 'dp'), 'mp'), parts along dimension 0
The draws below stay inside these ranges and needn't reach their ends.
There are 2 independent parts, one for each index of `groups`. The reference program is written for one: setup_inputs(seed, part) draws one part's arguments, and reference() takes and returns one part's arrays. A program takes and returns all parts, laid end to end along the dimension named above; an argument that names none is the same for every part. Nothing has to cross between parts.
All inputs are finite; a program needn't handle non-finite values.
Results may differ from the reference program's by a relative error of at most 0.014.
The reference program's roundings to bfloat16 on the way (of `rot_low`, `turned`, `centres` and `picked`) count: a program that leaves them out, or rounds other values in their place, can miss the bound.
Values may be sent and summed in bfloat16 or wider, within the bound.
A program may use at most 64 MiB of HBM per device.

```python
import math
import jax
import jax.numpy as jnp
from jax import lax

D = 1024
SUB = 64
K = 256
ALTS = 2
NS_STEPS = 5
M = 16
ROWS = 8192


def draw_embeddings(key, part):
    key = jax.random.fold_in(key, 11)
    key_rows, key_cols, key_base = jax.random.split(key, 3)
    row_scale = jnp.exp(jax.random.uniform(key_rows, (ROWS, 1), jnp.float32, math.log(0.3), math.log(3.0)))
    jitter = jax.random.uniform(key_cols, (1, D), jnp.float32, -0.4, 0.4)
    place = jnp.arange(D, dtype=jnp.float32).reshape(1, D) / (D - 1.0)
    ramp = math.log(0.5) + place * (math.log(2.0) - math.log(0.5))
    col_scale = jnp.exp(ramp + jitter)
    values = row_scale * col_scale * jax.random.normal(key_base, (ROWS, D), jnp.float32)
    values = jnp.clip(values, -60.0, 60.0)
    return values.astype(jnp.bfloat16)


def set_ends(drawn, own_key, smallest, largest):
    index_at = [jax.random.randint(jax.random.fold_in(own_key, axis), (), 0, length) for axis, length in enumerate(drawn.shape)]
    longest = drawn.shape.index(max(drawn.shape))
    beside = index_at[:longest] + [(index_at[longest] + 1) % drawn.shape[longest]] + index_at[longest + 1:]
    return drawn.at[tuple(index_at)].set(smallest).at[tuple(beside)].set(largest)


def levels(own_key, shape, cuts, least, top_value):
    def one(axis_at, shards_of):
        steps = jax.random.uniform(jax.random.fold_in(jax.random.fold_in(own_key, 6), axis_at), (shards_of,), jnp.float32, least / len(cuts), top_value / len(cuts))
        return jnp.repeat(jnp.exp(steps), shape[axis_at] // shards_of).reshape((-1,) + (1,) * (len(shape) - axis_at - 1))

    level = one(*cuts[0])
    for cut in cuts[1:]:
        level = level * one(*cut)
    return level


def centred(own_key, extent, scale, most, cuts=(), held_as=jnp.bfloat16):
    values = jax.random.normal(own_key, extent, jnp.float32) * scale
    if len(cuts) > 0:
        values = levels(own_key, extent, cuts, -0.22, 0.18) * values
    return jnp.clip(values, min=-most, max=most).astype(held_as)


def setup_inputs(seed: int = 0, part: int = 0) -> dict:
    streams_of = jax.random.split(jax.random.key(seed), 4)
    own_keys = jax.random.split(jax.random.fold_in(streams_of[3], part), 4)
    embeddings = draw_embeddings(jax.random.fold_in(jax.random.fold_in(streams_of[3], part), 71), part)
    rotation = centred(streams_of[1], (D, D), D ** -0.5, 0.1875, ((1, 4),))
    codes = set_ends(jax.random.randint(own_keys[2], (ALTS, ROWS, M), 0, K), jax.random.fold_in(own_keys[2], 1), 0, K - 1).astype(jnp.int32)
    return {"embeddings": embeddings, "rotation": rotation, "codes": codes}


coef_one = 3.4445
coef_two = -4.775
coef_three = 2.0315

def reference(embeddings, rotation, codes):
    rot_low = rotation
    ones_col = jnp.ones((ROWS,), jnp.float32)
    centres = jnp.zeros((K, M, SUB), jnp.bfloat16)
    polar = jnp.zeros((D, D), jnp.float32)
    highest = lax.Precision.HIGHEST
    for alternation in range(ALTS):
        labels = codes[alternation]
        turned = jnp.dot(embeddings, rot_low, preferred_element_type=jnp.float32).astype(jnp.bfloat16)
        pieces = turned.astype(jnp.float32).reshape(ROWS, M, SUB)
        class_sum = jax.vmap(lambda piece, label: jax.ops.segment_sum(piece, label, num_segments=K), in_axes=(1, 1), out_axes=1)(pieces, labels)
        class_count = jax.vmap(lambda label: jax.ops.segment_sum(ones_col, label, num_segments=K), in_axes=1, out_axes=1)(labels)
        centres = (class_sum / (class_count[:, :, None] + 1.0)).astype(jnp.bfloat16)
        picked = jax.vmap(lambda table, label: table[label], in_axes=(1, 1), out_axes=1)(centres, labels).reshape(ROWS, D)
        cross = lax.dot_general(embeddings, picked, (((0,), (0,)), ((), ())), preferred_element_type=jnp.float32)
        polar = cross / (jnp.sqrt(jnp.sum(cross * cross)) + 1e-06)
        for iterate in range(NS_STEPS):
            gram = jnp.dot(polar.T, polar, precision=highest, preferred_element_type=jnp.float32)
            first_prod = jnp.dot(polar, gram, precision=highest, preferred_element_type=jnp.float32)
            second_prod = jnp.dot(first_prod, gram, precision=highest, preferred_element_type=jnp.float32)
            polar = coef_one * polar + coef_two * first_prod + coef_three * second_prod
        rot_low = polar.astype(jnp.bfloat16)
    rotated = jnp.dot(embeddings, rot_low, preferred_element_type=jnp.float32).astype(jnp.bfloat16)
    return (centres.reshape(K, D), polar, rotated)
```

```python
import functools

import jax
import jax.numpy as jnp
from jax import lax
from jax.experimental import pallas as pl
from jax.experimental.pallas import tpu as pltpu
from jax.sharding import PartitionSpec as P

SUB = 64
K = 256
ALTS = 2
NS_STEPS = 5
LOW_STEPS = 2
BLOCK = 512

coef_one = 3.4445
coef_two = -4.775
coef_three = 2.0315

TN = (((0,), (0,)), ((), ()))
NN = (((1,), (0,)), ((), ()))
NT = (((1,), (1,)), ((), ()))


def mul(one, two, dims):
    return lax.dot_general(one, two, dims, preferred_element_type=jnp.float32)


def split(value):
    high = value.astype(jnp.bfloat16)
    low = (value - high.astype(jnp.float32)).astype(jnp.bfloat16)
    return high, low


def mul3(one, two, dims):
    return mul(one[1], two[0], dims) + mul(one[0], two[1], dims) + mul(one[0], two[0], dims)


def polar_kernel(own, cross_ref, out_ref, turn_high, turn_low, gram_high, gram_low, ser_high, ser_low):
    width = cross_ref.shape[0]
    halves = width // BLOCK
    total = jnp.sum(cross_ref[...] * cross_ref[...])
    scale = 1.0 / (jnp.sqrt(jnp.full((1, 1), total, jnp.float32)) + 1e-06)

    def at(tile):
        row = pl.ds(pl.multiple_of((tile // halves) * BLOCK, BLOCK), BLOCK)
        col = pl.ds(pl.multiple_of((tile % halves) * BLOCK, BLOCK), BLOCK)
        return row, col

    def put(high_ref, low_ref, lead, value):
        high, low = split(value)
        high_ref[lead] = high
        if low_ref is not None:
            low_ref[lead] = low

    @pl.loop(0, halves * halves)
    def _(tile):
        row, col = at(tile)
        high, low = split(cross_ref[row, col] * scale)
        turn_high[0, row, col] = high
        turn_low[0, row, col] = low

    for iterate in range(NS_STEPS - 1):
        now, later = iterate % 2, (iterate + 1) % 2
        fine = iterate >= LOW_STEPS

        @pl.loop(0, halves * halves)
        def _(tile):
            row, col = at(tile)
            if fine:
                gram = mul3(
                    (turn_high[now, row, :], turn_low[now, row, :]),
                    (turn_high[now, col, :], turn_low[now, col, :]),
                    NT,
                )
                gram_high[row, col], gram_low[row, col] = split(gram)
            else:
                gram = mul(turn_high[now, row, :], turn_high[now, col, :], NT)
                gram_high[row, col] = gram.astype(jnp.bfloat16)

        @pl.loop(0, halves * halves)
        def _(tile):
            row, col = at(tile)
            if fine:
                square = mul3(
                    (gram_high[row, :], gram_low[row, :]), (gram_high[:, col], gram_low[:, col]), NN
                )
                gram = gram_high[row, col].astype(jnp.float32) + gram_low[row, col].astype(jnp.float32)
                series = coef_two * gram + coef_three * square
                ser_high[row, col], ser_low[row, col] = split(series)
            else:
                square = mul(gram_high[row, :], gram_high[:, col], NN)
                gram = gram_high[row, col].astype(jnp.float32)
                ser_high[row, col] = (coef_two * gram + coef_three * square).astype(jnp.bfloat16)

        @pl.loop(0, halves * halves)
        def _(tile):
            row, col = at(tile)
            turn = turn_high[now, row, col].astype(jnp.float32) + turn_low[now, row, col].astype(
                jnp.float32
            )
            if fine:
                step = mul3(
                    (ser_high[row, :], ser_low[row, :]),
                    (turn_high[now, :, col], turn_low[now, :, col]),
                    NN,
                )
            else:
                step = mul(ser_high[row, :], turn_high[now, :, col], NN)
            high, low = split(coef_one * turn + step)
            turn_high[later, row, col] = high
            turn_low[later, row, col] = low

    now = (NS_STEPS - 1) % 2
    mine = pl.ds(pl.multiple_of(lax.axis_index("mp") * own, own), own)
    whole = (turn_high.at[now], turn_low.at[now])
    base = (whole[0][mine, :], whole[1][mine, :])

    def by_blocks(left, dims):
        parts = []
        for start in range(0, width, BLOCK):
            part = slice(start, start + BLOCK)
            if dims is NT:
                right = (whole[0][part, :], whole[1][part, :])
            else:
                right = (whole[0][:, part], whole[1][:, part])
            parts.append(mul3(left, right, dims))
        return jnp.concatenate(parts, axis=1)

    gram = by_blocks(base, NT)
    first = by_blocks(split(gram), NN)
    square = by_blocks(split(first), NT)
    series = coef_two * gram + coef_three * square
    step = by_blocks(split(series), NN)
    turn = base[0].astype(jnp.float32) + base[1].astype(jnp.float32)
    out_ref[...] = coef_one * turn + step


def polar_rows(cross, own):
    width = cross.shape[0]
    square = (width, width)
    return pl.pallas_call(
        functools.partial(polar_kernel, own),
        out_shape=jax.ShapeDtypeStruct((own, width), jnp.float32),
        in_specs=[pl.BlockSpec(memory_space=pltpu.VMEM)],
        out_specs=pl.BlockSpec(memory_space=pltpu.VMEM),
        scratch_shapes=[
            pltpu.VMEM((2,) + square, jnp.bfloat16),
            pltpu.VMEM((2,) + square, jnp.bfloat16),
            pltpu.VMEM(square, jnp.bfloat16),
            pltpu.VMEM(square, jnp.bfloat16),
            pltpu.VMEM(square, jnp.bfloat16),
            pltpu.VMEM(square, jnp.bfloat16),
        ],
        compiler_params=pltpu.CompilerParams(vmem_limit_bytes=48 * 1024 * 1024),
        cost_estimate=pl.CostEstimate(
            flops=60 * width * width * width, bytes_accessed=8 * width * width, transcendentals=0
        ),
        name="polar_steps",
    )(cross)


def body(embeddings, rotation, codes):
    col_count = rotation.shape[1]
    width = rotation.shape[0]
    local_subs = col_count // SUB
    row_count = embeddings.shape[0]
    levels = jnp.arange(K, dtype=jnp.int32)
    dp_at = lax.axis_index("dp")
    tile_rows = width // lax.axis_size("dp")
    turn_rows = None
    for alternation in range(ALTS):
        if alternation == 0:
            turned = mul(embeddings, rotation, NN).astype(jnp.bfloat16)
        else:
            turned = mul(embeddings, turn_rows.astype(jnp.bfloat16), NT).astype(jnp.bfloat16)
        selector = (codes[alternation][:, :, None] == levels).astype(jnp.bfloat16)
        pieces = turned.reshape(row_count, local_subs, SUB)
        class_sum = jnp.einsum("rlk,rls->kls", selector, pieces, preferred_element_type=jnp.float32)
        class_count = jnp.sum(selector, axis=0, dtype=jnp.float32).T
        class_sum, class_count = lax.psum((class_sum, class_count), "dp")
        centres = (class_sum / (class_count[:, :, None] + 1.0)).astype(jnp.bfloat16)
        picked = jnp.einsum("rlk,kls->rls", selector, centres, preferred_element_type=jnp.float32)
        picked = picked.astype(jnp.bfloat16).reshape(row_count, col_count)
        cross_part = mul(picked, embeddings, TN)
        cross_tile = lax.psum_scatter(cross_part, "dp", scatter_dimension=0, tiled=True)
        cross = lax.all_gather(cross_tile, ("mp", "dp"), axis=0, tiled=True)
        turn_rows = polar_rows(cross, col_count)
    rotated = mul(embeddings, turn_rows.astype(jnp.bfloat16), NT).astype(jnp.bfloat16)
    polar_tile = lax.dynamic_slice_in_dim(turn_rows, dp_at * tile_rows, tile_rows, 1).T
    return (centres.reshape(K, col_count), polar_tile, rotated)


def solution(mesh):
    placed = (P(("groups", "dp"), None), P(None, "mp"), P(None, ("groups", "dp"), "mp"))
    return jax.shard_map(
        body,
        mesh=mesh,
        in_specs=placed,
        out_specs=(P("groups", "mp"), P(("groups", "dp"), "mp"), P(("groups", "dp"), "mp")),
        check_vma=False,
    )
```
